256 devices in a mesh: replica: 16 (over x, z_lo), shard: 16 (over y, z_hi, core).
Axes of the slice: x: 4, y: 4, z: 8 (z_hi: 2, z_lo: 4; z = z_hi * 4 + z_lo), core: 2. Of those that a mesh axis runs over, the one named last changes fastest.
Arguments:
- tokens: bfloat16 [131072, 4096], P(('replica', 'shard')), may hold values from -24 to 24
- norm_gain: float32 [4096], replicated, may hold values from 0.1 to 1.9
- weight_values: bfloat16 [32, 128, 1024], P('shard'), may hold values from -0.09375 to 0.09375
- weight_scales: float32 [32, 8], P('shard'), may hold values from 0.5 to 2
- grad_projected: bfloat16 [131072, 1024], P(('replica', 'shard')), may hold values from -6 to 6
Outputs:
- projected: bfloat16 [131072, 1024], P(('replica', 'shard'))
- grad_tokens: bfloat16 [131072, 4096], P(('replica', 'shard'))
- grad_weight: float32 [32, 128, 1024], P('shard')
The draws below stay inside these ranges and needn't reach their ends.
All inputs are finite; a program needn't handle non-finite values.
Results may differ from the reference program's by a relative error of at most 0.027.
Values may be sent and summed in bfloat16 or wider, within the bound.
No kernel may reach another device: no remote copies, remote signals or barrier semaphores. Data moves between devices by JAX's collectives and lax.ppermute only.
A program may use at most 128 MiB of HBM per device.

```python
import math
import jax
import jax.numpy as jnp
from jax import lax

D = 4096
KVH = 4
HD = 128
BLK = 128
TOK_DEV = 512
TOKENS = 131072
N_REPLICA = 16
N_SHARD = 16


def with_spikes(array, own_key, source, target, shards_of, factor):
    def block_of(dim):
        return (jnp.arange(array.shape[dim]) // (array.shape[dim] // shards_of)).reshape((-1,) + (1,) * (array.ndim - 1 - dim))

    one_side = jax.random.permutation(own_key, shards_of)[block_of(target)]
    second = (block_of(target) + shards_of // 2) % shards_of
    return jnp.where((block_of(source) == one_side) | (block_of(source) == second), factor * array, array)


def level_of(own_key, shape, shards, low, top_value):
    def one(axis_at, parts):
        draws = jax.random.uniform(jax.random.fold_in(jax.random.fold_in(own_key, 6), axis_at), (parts,), jnp.float32, low / len(shards), top_value / len(shards))
        return jnp.repeat(jnp.exp(draws), shape[axis_at] // parts).reshape((-1,) + (1,) * (len(shape) - axis_at - 1))

    factor_of = one(*shards[0])
    for cut in shards[1:]:
        factor_of = factor_of * one(*cut)
    return factor_of


def scatter_about(stream_key, dims, spread, reach, shards=(), kind=jnp.bfloat16):
    factor_of = level_of(stream_key, dims, shards, -0.22, 0.18) if shards else 1.0
    drawn = jax.random.normal(stream_key, dims, jnp.float32) * spread * factor_of
    return jnp.minimum(jnp.maximum(drawn, -reach), reach).astype(kind)


def gaussian_with(stream_key, extent, scale, most, pieces, heavy, kind=jnp.bfloat16):
    result = scale * jax.random.normal(stream_key, extent, jnp.float32)
    if pieces:
        result = result * level_of(stream_key, extent, pieces, -0.22, 0.18)
    return jnp.clip(with_spikes(result, jax.random.fold_in(stream_key, 3), *heavy), -most, most).astype(kind)


def setup_inputs(seed: int = 0) -> dict:
    key_of = jax.random.split(jax.random.key(seed), 6)
    tokens = gaussian_with(key_of[0], (TOKENS, D), 1.0, 24.0, ((0, 256),), (0, 1, 256, 6.0))
    norm_gain = jnp.clip(1.0 + 0.18 * jax.random.normal(key_of[1], (D,), jnp.float32), 0.1, 1.9)
    weight_values = scatter_about(key_of[2], (D // BLK, BLK, 2 * KVH * HD), D ** -0.5, 0.09375, ((0, 16),))
    weight_scales = jnp.clip(jnp.exp(math.log(2.0) - 1.3862944 * jax.random.uniform(key_of[3], (D // BLK, 2 * KVH * HD // BLK), jnp.float32) ** level_of(key_of[3], (D // BLK, 2 * KVH * HD // BLK), ((0, 16),), -0.2, 0.2)), 0.5, 2.0)
    grad_projected = scatter_about(key_of[4], (TOKENS, 2 * KVH * HD), 1.0, 6.0, ((0, 256),))
    return dict(tokens=tokens, norm_gain=norm_gain, weight_values=weight_values, weight_scales=weight_scales, grad_projected=grad_projected)


def dequantize(values, scales):
    block_rows = values.shape[1]
    widened = jnp.repeat(scales, block_rows, axis=1)
    scaled = (values.astype(jnp.float32) * widened[:, None, :]).astype(jnp.bfloat16)
    return scaled.reshape(values.shape[0] * block_rows, values.shape[2])

def rope_tables(rows_here, head_size):
    half_size = head_size // 2
    position = jnp.arange(rows_here, dtype=jnp.float32)
    inverse = jnp.exp(-jnp.arange(half_size, dtype=jnp.float32) * (2.0 * math.log(500000.0) / head_size))
    angles = position[:, None] * inverse[None, :]
    return (jnp.cos(angles), jnp.sin(angles))

def rotate(key_part, cosine, sine_part, head_size, backward):
    rows_here = key_part.shape[0]
    half_size = head_size // 2
    shaped = key_part.reshape(rows_here, -1, 2, half_size)
    first_half = shaped[:, :, 0, :]
    second_half = shaped[:, :, 1, :]
    cos_b = cosine[:, None, :]
    sin_b = sine_part[:, None, :]
    if backward:
        new_first = first_half * cos_b + second_half * sin_b
        new_second = second_half * cos_b - first_half * sin_b
    else:
        new_first = first_half * cos_b - second_half * sin_b
        new_second = second_half * cos_b + first_half * sin_b
    return jnp.stack([new_first, new_second], axis=2).reshape(rows_here, -1)

def local_pass(tok_block, grad_block, norm_gain, weight, cosine, sine_part):
    key_width = weight.shape[1] // 2
    inputs = tok_block.astype(jnp.float32)
    rstd = lax.rsqrt(lax.optimization_barrier(jnp.mean(inputs * inputs, axis=-1, keepdims=True)) + 1e-05)
    hat = inputs * rstd
    normed = (hat * norm_gain[None, :]).astype(jnp.bfloat16)
    raw = jnp.dot(normed, weight, preferred_element_type=jnp.float32)
    rotated = rotate(raw[:, :key_width], cosine, sine_part, HD, False)
    projected = jnp.concatenate([rotated, raw[:, key_width:]], axis=1).astype(jnp.bfloat16)
    grad_keys = rotate(grad_block[:, :key_width].astype(jnp.float32), cosine, sine_part, HD, True)
    grad_pair = jnp.concatenate([grad_keys, grad_block[:, key_width:].astype(jnp.float32)], axis=1).astype(jnp.bfloat16)
    grad_normed = lax.dot_general(grad_pair, weight, (((1,), (1,)), ((), ())), preferred_element_type=jnp.float32)
    grad_hat = grad_normed * norm_gain[None, :]
    grad_tokens = (rstd * (grad_hat - hat * lax.optimization_barrier(jnp.mean(grad_hat * hat, axis=-1, keepdims=True)))).astype(jnp.bfloat16)
    partial_value = lax.dot_general(normed, grad_pair, (((0,), (0,)), ((), ())), preferred_element_type=jnp.float32)
    return (projected, grad_tokens, partial_value)

def reference(tokens, norm_gain, weight_values, weight_scales, grad_projected):
    weight = dequantize(weight_values, weight_scales)
    pair_width = 2 * KVH * HD
    cosine, sine_part = rope_tables(TOK_DEV, HD)
    tok_blocks = tokens.reshape(N_REPLICA, N_SHARD, TOK_DEV, D)
    grad_blocks = grad_projected.reshape(N_REPLICA, N_SHARD, TOK_DEV, pair_width)

    def replica_step(summed_total, inputs_pair):

        def shard_step(running, inner_pair):
            projected, grad_tokens, partial_value = local_pass(inner_pair[0], inner_pair[1], norm_gain, weight, cosine, sine_part)
            rounded = lax.optimization_barrier(partial_value.astype(jnp.bfloat16))
            return (running + rounded.astype(jnp.float32), (projected, grad_tokens))
        running, outputs = lax.scan(shard_step, jnp.zeros((D, pair_width), jnp.float32), inputs_pair)
        rounded = lax.optimization_barrier(running.astype(jnp.bfloat16))
        return (summed_total + rounded.astype(jnp.float32), outputs)
    summed_total, outputs = lax.scan(replica_step, jnp.zeros((D, pair_width), jnp.float32), (tok_blocks, grad_blocks))
    projected = outputs[0].reshape(TOKENS, pair_width)
    grad_tokens = outputs[1].reshape(TOKENS, D)
    grad_weight = (summed_total * (1.0 / math.sqrt(TOKENS))).reshape(D // BLK, BLK, pair_width)
    return (projected, grad_tokens, grad_weight)
```

```python
import math

import jax
import jax.numpy as jnp
from jax import lax
from jax.experimental import pallas as pl
from jax.experimental.pallas import tpu as pltpu
from jax.sharding import PartitionSpec as P

HD = 128
AXES = ("replica", "shard")
F32 = jnp.float32
BF16 = jnp.bfloat16
NX, NY, NZL = 4, 4, 4
VMEM_LIMIT = 56 * 1024 * 1024


def place(device):
    replica, shard = divmod(device, 16)
    return replica // 4, shard // 4, (shard // 2 % 2) * 4 + replica % 4, shard % 2


def device_at(x, y, z, core):
    return ((x % 4) * 4 + z % 4) * 16 + (y % 4) * 4 + (z // 4) * 2 + core


def send(array, move):
    pairs = [(d, device_at(*move(*place(d)))) for d in range(256)]
    return lax.ppermute(array, AXES, pairs)


def to_x(array, step):
    return send(array, lambda x, y, z, c: (x + step, y, z, c))


def to_y(array, step):
    return send(array, lambda x, y, z, c: (x, y + step, z, c))


def to_core(array):
    return send(array, lambda x, y, z, c: (x, y, z, 1 - c))


def to_mirror(array):
    return send(array, lambda x, y, z, c: (x, y, 7 - z, c))


def to_zlo(array, flip):
    return send(array, lambda x, y, z, c: (x, y, (z // 4) * 4 + (z % 4 ^ flip), c))


def rope_tables(rows_here, head_size):
    half_size = head_size // 2
    position = jnp.arange(rows_here, dtype=F32)
    inverse = jnp.exp(-jnp.arange(half_size, dtype=F32) * (2.0 * math.log(500000.0) / head_size))
    angles = position[:, None] * inverse[None, :]
    cosine, sine = jnp.cos(angles), jnp.sin(angles)
    return jnp.concatenate([cosine, cosine], axis=1), jnp.concatenate([-sine, sine], axis=1)


def block_of(where, dy, dzh, dc):
    y, zh, c = where[1], where[2], where[3]
    return ((y + dy) % 4) * 4 + (zh ^ dzh) * 2 + (c ^ dc)


def aligned(start):
    return pl.ds(pl.multiple_of(start * 256, 256), 256)


def prologue_kernel(where, tok_ref, gain_ref, gproj_ref, cos_ref, sin_ref, normed_ref, rstd_ref, pair_ref):
    rows = tok_ref.shape[0]
    total = jnp.zeros((rows, 1), F32)
    for b in range(16):
        part = tok_ref[:, b * 256 : (b + 1) * 256].astype(F32)
        total = total + jnp.sum(part * part, axis=1, keepdims=True)
    rstd = lax.rsqrt(total * (1.0 / 4096) + 1e-05)
    rstd_ref[...] = jnp.broadcast_to(rstd, (rows, 128))
    for q in range(4):
        for dy in range(4):
            cols = aligned(block_of(where, dy, q // 2, q % 2))
            part = tok_ref[:, cols].astype(F32)
            normed_ref[q, :, dy * 256 : (dy + 1) * 256] = (part * rstd * gain_ref[:, cols]).astype(BF16)
    for h in range(4):
        cols = slice(h * 128, (h + 1) * 128)
        g = gproj_ref[:, cols].astype(F32)
        pair_ref[:, cols] = (g * cos_ref[...] - pltpu.roll(g, 64, 1) * sin_ref[...]).astype(BF16)
    pair_ref[:, 512:] = gproj_ref[:, 512:]


def prologue(where, tokens, gain, gproj, cos2, sin2):
    rows = 128
    row = lambda i, where: (i, 0)
    return pl.pallas_call(
        prologue_kernel,
        grid_spec=pltpu.PrefetchScalarGridSpec(
            num_scalar_prefetch=1,
            grid=(512 // rows,),
            in_specs=[
                pl.BlockSpec((rows, 4096), row),
                pl.BlockSpec((1, 4096), lambda i, where: (0, 0)),
                pl.BlockSpec((rows, 1024), row),
                pl.BlockSpec((rows, 128), row),
                pl.BlockSpec((rows, 128), row),
            ],
            out_specs=[
                pl.BlockSpec((4, rows, 1024), lambda i, where: (0, i, 0)),
                pl.BlockSpec((rows, 128), row),
                pl.BlockSpec((rows, 1024), row),
            ],
        ),
        out_shape=[
            jax.ShapeDtypeStruct((4, 512, 1024), BF16),
            jax.ShapeDtypeStruct((512, 128), F32),
            jax.ShapeDtypeStruct((512, 1024), BF16),
        ],
        compiler_params=pltpu.CompilerParams(vmem_limit_bytes=VMEM_LIMIT),
        cost_estimate=pl.CostEstimate(flops=20_000_000, bytes_accessed=10 << 20, transcendentals=0),
        name="prologue",
    )(where, tokens, gain, gproj, cos2, sin2)


def grad_kernel(by_x, has_other, where, n_ref, pair_ref, *refs):
    out_ref = refs[-1]
    if by_x:
        pair = pair_ref[:, aligned((where[0] + pl.program_id(0)) % 4)]
    else:
        pair = pair_ref[...]
    got = lax.dot_general(n_ref[0], pair, (((0,), (0,)), ((), ())), preferred_element_type=F32)
    if has_other:
        got = got + refs[0][0].astype(F32)
    out_ref[0] = got.astype(BF16)


def grad_part(where, normed, pair, q, other=None):
    by_x = q >= 2
    if by_x:
        shape = (4, 1024, 256)
        n_spec = pl.BlockSpec((1, 512, 1024), lambda i, where: (q, 0, 0))
    else:
        shape = (4, 256, 1024)
        n_spec = pl.BlockSpec((1, 512, 256), lambda i, where: (q, 0, i))
    step = pl.BlockSpec((1,) + shape[1:], lambda i, where: (i, 0, 0))
    others = [] if other is None else [other]
    return pl.pallas_call(
        lambda *refs: grad_kernel(by_x, bool(others), *refs),
        grid_spec=pltpu.PrefetchScalarGridSpec(
            num_scalar_prefetch=1,
            grid=(4,),
            in_specs=[n_spec, pl.BlockSpec((512, 1024), lambda i, where: (0, 0))] + [step] * len(others),
            out_specs=step,
        ),
        out_shape=jax.ShapeDtypeStruct(shape, BF16),
        compiler_params=pltpu.CompilerParams(vmem_limit_bytes=VMEM_LIMIT),
        cost_estimate=pl.CostEstimate(flops=2 * 512 * 1024 * 1024, bytes_accessed=4 << 20, transcendentals=0),
        name="grad_part",
    )(where, normed, pair, *others)


def main_kernel(where, *refs):
    near = [refs[0:4], refs[4:8]]
    far = [refs[8:12], refs[12:16]]
    normed_ref, tok_ref, pair_ref, rstd_ref, gain_ref, cos_ref, sin_ref = refs[16:23]
    proj_ref, gtok_ref, raw_ref = refs[23:26]
    for n in range(4):
        cols = slice(n * 256, (n + 1) * 256)
        acc = None
        for dc in range(2):
            for dy in range(4):
                term = jnp.dot(
                    normed_ref[dc, :, dy * 256 : (dy + 1) * 256],
                    near[dc][dy][:, cols],
                    preferred_element_type=F32,
                )
                acc = term if acc is None else acc + term
        raw_ref[:, cols] = acc
    for dx in range(4):
        cols = aligned((where[0] + dx) % 4)
        acc = raw_ref[:, cols]
        for dc in range(2):
            acc = acc + jnp.dot(normed_ref[2 + dc], far[dc][dx][...], preferred_element_type=F32)
        raw_ref[:, cols] = acc
    dots = jnp.zeros((512, 128), F32)
    for n in range(8):
        cols = slice(n * 128, (n + 1) * 128)
        raw = raw_ref[:, cols]
        dots = dots + raw * pair_ref[:, cols].astype(F32)
        if n < 4:
            raw = raw * cos_ref[...] + pltpu.roll(raw, 64, 1) * sin_ref[...]
        proj_ref[:, cols] = raw.astype(BF16)
    mean = jnp.sum(dots, axis=1, keepdims=True) * (1.0 / 4096)
    rstd = rstd_ref[:, 0:1]
    tail = mean * rstd * rstd
    for q in range(4):
        for dy in range(4):
            dc = q % 2
            if q < 2:
                acc = lax.dot_general(
                    pair_ref[...], near[dc][dy][...], (((1,), (1,)), ((), ())), preferred_element_type=F32
                )
            else:
                acc = None
                for dx in range(4):
                    term = lax.dot_general(
                        pair_ref[:, aligned((where[0] + dx) % 4)],
                        far[dc][dx][dy * 256 : (dy + 1) * 256, :],
                        (((1,), (1,)), ((), ())),
                        preferred_element_type=F32,
                    )
                    acc = term if acc is None else acc + term
            cols = aligned(block_of(where, dy, q // 2, dc))
            gtok_ref[:, cols] = (
                acc * gain_ref[:, cols] * rstd - tok_ref[:, cols].astype(F32) * tail
            ).astype(BF16)


def main_part(where, near, far, normed, tokens, pair, rstd, gain, cos2, sin2):
    args = (*near, *far, normed, tokens, pair, rstd, gain, cos2, sin2)
    whole = lambda a: pl.BlockSpec(a.shape, lambda i, where, n=a.ndim: (0,) * n)
    return pl.pallas_call(
        main_kernel,
        grid_spec=pltpu.PrefetchScalarGridSpec(
            num_scalar_prefetch=1,
            grid=(1,),
            in_specs=[whole(a) for a in args],
            out_specs=[
                pl.BlockSpec((512, 1024), lambda i, where: (0, 0)),
                pl.BlockSpec((512, 4096), lambda i, where: (0, 0)),
            ],
            scratch_shapes=[pltpu.VMEM((512, 1024), F32)],
        ),
        out_shape=[jax.ShapeDtypeStruct((512, 1024), BF16), jax.ShapeDtypeStruct((512, 4096), BF16)],
        compiler_params=pltpu.CompilerParams(vmem_limit_bytes=VMEM_LIMIT),
        cost_estimate=pl.CostEstimate(flops=4 * 512 * 4096 * 1024, bytes_accessed=24 << 20, transcendentals=0),
        name="main_part",
    )(where, *args)


def total(parts):
    acc = parts[0].astype(F32)
    for part in parts[1:]:
        acc = acc + part.astype(F32)
    return acc.astype(BF16)


def on_device(tokens, norm_gain, weight_values, weight_scales, grad_projected):
    replica, shard = lax.axis_index("replica"), lax.axis_index("shard")
    x, y, zh, core = replica // 4, shard // 4, shard // 2 % 2, shard % 2
    where = jnp.stack([x, y, zh, core]).astype(jnp.int32)
    gain = norm_gain[None, :]
    widened = jnp.repeat(weight_scales, 128, axis=1)
    own = (weight_values.astype(F32) * widened[:, None, :]).astype(BF16).reshape(256, 1024)

    quarter = lax.dynamic_slice(own, (0, x * 256), (256, 256))
    quarter = to_mirror(quarter)
    near = [own] + [to_y(own, -dy) for dy in (1, 2, 3)]
    pack = jnp.concatenate([quarter] + [to_y(quarter, -dy) for dy in (1, 2, 3)], axis=0)
    far = [pack] + [to_x(pack, -dx) for dx in (1, 2, 3)]
    near = near + [to_core(a) for a in near]
    far = far + [to_core(a) for a in far]

    cos2, sin2 = rope_tables(512, HD)
    normed, rstd, pair = prologue(where, tokens, gain, grad_projected, cos2, sin2)

    far_got = to_core(grad_part(where, normed, pair, 3))
    near_got = to_core(grad_part(where, normed, pair, 1))
    far_sum = grad_part(where, normed, pair, 2, far_got)
    far_sum = total([far_sum[0]] + [to_x(far_sum[dx], dx) for dx in (1, 2, 3)]).reshape(4, 256, 256)
    near_sum = grad_part(where, normed, pair, 0, near_got)
    near_sum = total([near_sum[0]] + [to_y(near_sum[dy], dy) for dy in (1, 2, 3)])
    far_sum = total([far_sum[0]] + [to_y(far_sum[dy], dy) for dy in (1, 2, 3)])
    near_cut = [lax.dynamic_slice(near_sum, (0, (x + dx) % 4 * 256), (256, 256)) for dx in range(4)]
    near_cut = [near_cut[0]] + [to_x(near_cut[dx], dx) for dx in (1, 2, 3)]
    mine = total(near_cut + [to_mirror(far_sum)])
    mine = total([mine, to_zlo(mine, 1)])
    mine = total([mine, to_zlo(mine, 3)])
    quarters = [mine] + [to_x(mine, -dx) for dx in (1, 2, 3)]
    grad = jnp.zeros((256, 1024), BF16)
    for dx in range(4):
        grad = lax.dynamic_update_slice(grad, quarters[dx], (0, (x + dx) % 4 * 256))
    grad_weight = (grad.astype(F32) * (1.0 / math.sqrt(131072))).reshape(2, 128, 1024)

    projected, grad_tokens = main_part(where, near, far, normed, tokens, pair, rstd, gain, cos2, sin2)
    return (projected, grad_tokens, grad_weight)


def solution(mesh):
    return jax.shard_map(
        on_device,
        mesh=mesh,
        in_specs=(
            P(AXES, None),
            P(),
            P("shard", None, None),
            P("shard", None),
            P(AXES, None),
        ),
        out_specs=(
            P(AXES, None),
            P(AXES, None),
            P("shard", None, None),
        ),
        check_vma=False,
    )
```

```python
import math

import jax
import jax.numpy as jnp
import numpy as np
from jax import lax
from jax.experimental import pallas as pl
from jax.experimental.pallas import tpu as pltpu
from jax.sharding import PartitionSpec as P

HD = 128
AXES = ("replica", "shard")
F32 = jnp.float32
BF16 = jnp.bfloat16
NX, NY, NZL = 4, 4, 4


def place(device):
    replica, shard = divmod(device, 16)
    return replica // 4, shard // 4, (shard // 2 % 2) * 4 + replica % 4, shard % 2


def device_at(x, y, z, core):
    return ((x % 4) * 4 + z % 4) * 16 + (y % 4) * 4 + (z // 4) * 2 + core


def send(array, move):
    pairs = [(d, device_at(*move(*place(d)))) for d in range(256)]
    return lax.ppermute(array, AXES, pairs)


def to_x(array, step):
    return send(array, lambda x, y, z, c: (x + step, y, z, c))


def to_y(array, step):
    return send(array, lambda x, y, z, c: (x, y + step, z, c))


def to_core(array):
    return send(array, lambda x, y, z, c: (x, y, z, 1 - c))


def to_mirror(array):
    return send(array, lambda x, y, z, c: (x, y, 7 - z, c))


def to_zlo(array, flip):
    return send(array, lambda x, y, z, c: (x, y, (z // 4) * 4 + (z % 4 ^ flip), c))


def rope_tables(rows_here, head_size):
    half_size = head_size // 2
    position = np.arange(rows_here, dtype=np.float32)
    inverse = np.exp(-np.arange(half_size, dtype=np.float32) * np.float32(2.0 * math.log(500000.0) / head_size))
    angles = position[:, None] * inverse[None, :]
    cosine, sine = np.cos(angles), np.sin(angles)
    return jnp.asarray(np.concatenate([cosine, cosine, -sine, sine], axis=1), F32)


def block_of(where, dy, dzh, dc):
    y, zh, c = where[1], where[2], where[3]
    return ((y + dy) % 4) * 4 + (zh ^ dzh) * 2 + (c ^ dc)


def aligned(start):
    return pl.ds(pl.multiple_of(start * 256, 256), 256)


ROWS = 128


def prologue_kernel(where, tok_hbm, gproj_hbm, gain_hbm, rope_hbm, *refs):
    normed_refs, (rstd_ref, pair_ref, pair_t_ref, far_ref) = refs[:4], refs[4:8]
    tok_ref, gproj_ref, gain_ref, rope_ref, sems = refs[8:]
    small = [
        pltpu.make_async_copy(gain_hbm, gain_ref, sems.at[512 // ROWS, 0]),
        pltpu.make_async_copy(rope_hbm, rope_ref, sems.at[512 // ROWS, 1]),
    ]
    copies = []
    for i in range(512 // ROWS):
        rows = slice(i * ROWS, (i + 1) * ROWS)
        copies.append(pltpu.make_async_copy(tok_hbm.at[rows], tok_ref.at[rows], sems.at[i, 0]))
        copies.append(pltpu.make_async_copy(gproj_hbm.at[rows], gproj_ref.at[rows], sems.at[i, 1]))
    for copy in (*copies[:2], *small, *copies[2:]):
        copy.start()
    for copy in small:
        copy.wait()
    for i in range(512 // ROWS):
        rows = slice(i * ROWS, (i + 1) * ROWS)
        copies[2 * i].wait()
        copies[2 * i + 1].wait()
        total = jnp.zeros((ROWS, 128), F32)
        for b in range(32):
            part = tok_ref[rows, b * 128 : (b + 1) * 128].astype(F32)
            total = total + part * part
        rstd = lax.rsqrt(jnp.sum(total, axis=1, keepdims=True) * (1.0 / 4096) + 1e-05)
        rstd_ref[rows, :] = jnp.broadcast_to(rstd, (ROWS, 128))
        for q in range(4):
            for dy in range(4):
                cols = aligned(block_of(where, dy, q // 2, q % 2))
                part = tok_ref[rows, cols].astype(F32)
                normed_refs[q][rows, dy * 256 : (dy + 1) * 256] = (part * rstd * gain_ref[:, cols]).astype(BF16)
        for h in range(8):
            cols = slice(h * 128, (h + 1) * 128)
            pair = gproj_ref[rows, cols]
            if h < 4:
                g = pair.astype(F32)
                pair = (g * rope_ref[rows, :128] - pltpu.roll(g, 64, 1) * rope_ref[rows, 128:]).astype(BF16)
            pair_ref[rows, cols] = pair
            pair_t_ref[cols, rows] = pair.T
    other_grad_kernel(False, where, pair_t_ref, normed_refs[3], far_ref)


def prologue(where, tokens, gproj, gain, rope):
    outs = [jax.ShapeDtypeStruct((512, 1024), BF16)] * 4 + [
        jax.ShapeDtypeStruct((512, 128), F32),
        jax.ShapeDtypeStruct((512, 1024), BF16),
        jax.ShapeDtypeStruct((1024, 512), BF16),
        jax.ShapeDtypeStruct((4, 4, 256, 256), BF16),
    ]
    given = (tokens, gproj, gain, rope)
    scratch = [jax.ShapeDtypeStruct(a.shape, a.dtype) for a in given]
    return call(prologue_kernel, "prologue", 0, where, (), outs, (), scratch, given, (512 // ROWS + 1, 2))


def cost(products, mib):
    flops = products * 2 * 512 * 1024 * 1024
    return pl.CostEstimate(flops=flops, bytes_accessed=(mib << 20) if flops else 1024, transcendentals=0)


def call(kernel, name, products, where, args, outs, ties=(), scratch=(), hbm=(), sems=None, out_hbm=False):
    many, kept = len(args) + len(hbm), len(args) + len(hbm) + len(ties)
    size = sum(a.size * a.dtype.itemsize for a in scratch)

    def body(where, *refs):
        kernel(where, *refs[:many], *refs[kept:])

    return pl.pallas_call(
        body,
        in_specs=[pl.BlockSpec(memory_space=pltpu.SMEM)]
        + [pl.BlockSpec(memory_space=pltpu.VMEM)] * len(args)
        + [pl.BlockSpec(memory_space=pltpu.HBM)] * len(hbm)
        + [pl.BlockSpec(memory_space=pl.ANY)] * len(ties),
        out_specs=[
            pl.BlockSpec(memory_space=pltpu.HBM if out_hbm and i == 0 else pltpu.VMEM) for i in range(len(outs))
        ],
        out_shape=outs,
        scratch_shapes=[pltpu.VMEM(a.shape, a.dtype) for a in scratch]
        + ([] if sems is None else [pltpu.SemaphoreType.DMA(sems)]),
        compiler_params=pltpu.CompilerParams(vmem_limit_bytes=size + (8 << 20)),
        cost_estimate=cost(products, size >> 20),
        name=name,
    )(where, *args, *hbm, *ties)


def grad_block(where, pair_t_ref, n_ref, near, d):
    if near:
        return jnp.dot(pair_t_ref[...], n_ref[:, d * 256 : (d + 1) * 256], preferred_element_type=F32)
    return jnp.dot(pair_t_ref[aligned((where[0] + d) % 4), :], n_ref[...], preferred_element_type=F32)


def other_grad_kernel(near, where, pair_t_ref, n_ref, out_ref):
    for d in range(4):
        got = grad_block(where, pair_t_ref, n_ref, near, d)
        if near:
            out_ref[d] = got.astype(BF16)
        else:
            for dy in range(4):
                out_ref[d, dy] = got[:, dy * 256 : (dy + 1) * 256].astype(BF16)


def other_near(where, pair_t, normed, ties):
    outs = [jax.ShapeDtypeStruct((4, 1024, 256), BF16)]
    kernel = lambda *refs: other_grad_kernel(True, *refs)
    return call(kernel, "other_near", 0, where, (pair_t, normed), outs, ties)[0]


def far_grad_kernel(where, pair_t_ref, n_ref, got_ref, own_ref, *refs):
    refs[4][...] = own_ref[...]
    for dx in range(4):
        got = grad_block(where, pair_t_ref, n_ref, False, dx)
        for dy in range(4):
            part = got[:, dy * 256 : (dy + 1) * 256] + got_ref[dx, dy].astype(F32)
            refs[dx][dy] = part.astype(BF16)


def far_grad(where, pair_t, normed, got, own, ties):
    outs = [jax.ShapeDtypeStruct((4, 256, 256), BF16)] * 4 + [jax.ShapeDtypeStruct(own.shape, BF16)]
    return call(far_grad_kernel, "far_grad", 1, where, (pair_t, normed, got, own), outs, ties)


def near_grad_first_kernel(where, pair_t_ref, n_ref, got_ref, quarter_ref, up_ref, down_ref, pass_ref):
    pass_ref[...] = quarter_ref[...]
    got = (grad_block(where, pair_t_ref, n_ref, True, 2) + got_ref[2].astype(F32)).astype(BF16)
    up_ref[...] = got[:512]
    down_ref[...] = got[512:]


def near_grad_first(where, pair_t, normed, got, quarter, ties):
    outs = [jax.ShapeDtypeStruct((512, 256), BF16)] * 2 + [jax.ShapeDtypeStruct(quarter.shape, BF16)]
    return call(near_grad_first_kernel, "near_grad_first", 0, where, (pair_t, normed, got, quarter), outs, ties)


def near_grad_rest_kernel(where, pair_t_ref, n_ref, got_ref, up_ref, down_ref, *refs):
    for slot, d in enumerate((1, 3, 0)):
        got = grad_block(where, pair_t_ref, n_ref, True, d) + got_ref[d].astype(F32)
        if d == 1:
            refs[slot][:512] = (got[:512] + up_ref[...].astype(F32)).astype(BF16)
            refs[slot][512:] = got[512:].astype(BF16)
        elif d == 3:
            refs[slot][:512] = got[:512].astype(BF16)
            refs[slot][512:] = (got[512:] + down_ref[...].astype(F32)).astype(BF16)
        else:
            refs[slot][...] = got.astype(BF16)


def near_grad_rest(where, pair_t, normed, got, up, down, ties):
    outs = [jax.ShapeDtypeStruct((1024, 256), BF16)] * 3
    return call(near_grad_rest_kernel, "near_grad_rest", 1, where, (pair_t, normed, got, up, down), outs, ties)


def join_kernel(where, *refs):
    start = 0
    for ref in refs[:-1]:
        refs[-1][start : start + ref.shape[0]] = ref[...]
        start += ref.shape[0]


def join(where, name, parts, ties=()):
    outs = [jax.ShapeDtypeStruct((sum(a.shape[0] for a in parts), parts[0].shape[1]), BF16)]
    return call(join_kernel, name, 0, where, parts, outs, ties)[0]


def forward_near_kernel(where, *refs):
    near, normed_refs, raw_ref = [refs[0:4], refs[4:8]], refs[8:10], refs[10]
    for n in range(4):
        cols = slice(n * 256, (n + 1) * 256)
        acc = None
        for dc in range(2):
            for dy in range(4):
                term = jnp.dot(
                    normed_refs[dc][:, dy * 256 : (dy + 1) * 256],
                    near[dc][dy][:, cols],
                    preferred_element_type=F32,
                )
                acc = term if acc is None else acc + term
        raw_ref[:, cols] = acc


def forward_near(where, near, normed, ties=()):
    outs = [jax.ShapeDtypeStruct((512, 1024), F32)]
    return call(forward_near_kernel, "forward_near", 2, where, (*near, *normed[:2]), outs, ties)[0]


def forward_far_kernel(where, *refs):
    far = [refs[0:4], refs[4:8]]
    normed_refs = refs[8:10]
    part_ref, pair_ref, rstd_ref, rope_ref, proj_ref, tail_ref, raw_ref = refs[10:]
    for dx in range(4):
        cols = aligned((where[0] + dx) % 4)
        acc = part_ref[:, cols]
        for dc in range(2):
            acc = acc + jnp.dot(normed_refs[dc][...], far[dc][dx][...], preferred_element_type=F32)
        raw_ref[:, cols] = acc
    dots = jnp.zeros((512, 128), F32)
    for n in range(8):
        cols = slice(n * 128, (n + 1) * 128)
        raw = raw_ref[:, cols]
        dots = dots + raw * pair_ref[:, cols].astype(F32)
        if n < 4:
            raw = raw * rope_ref[:, :128] + pltpu.roll(raw, 64, 1) * rope_ref[:, 128:]
        proj_ref[:, cols] = raw.astype(BF16)
    mean = jnp.sum(dots, axis=1, keepdims=True) * (1.0 / 4096)
    tail_ref[...] = mean * rstd_ref[...] * rstd_ref[...]


def forward_far(where, far, normed, part, pair, rstd, rope, ties=()):
    raw = jax.ShapeDtypeStruct((512, 1024), F32)
    return call(
        forward_far_kernel,
        "forward_far",
        2,
        where,
        (*far, *normed[2:], part, pair, rstd, rope),
        [jax.ShapeDtypeStruct((512, 1024), BF16), jax.ShapeDtypeStruct((512, 128), F32)],
        ties,
        [raw],
    )


def backward_kernel(where, *refs):
    near, far = [refs[0:4], refs[4:8]], [refs[8:12], refs[12:16]]
    pair_ref, tok_ref, rstd_ref, tail_ref, gain_ref, out_hbm, token_ref, out_ref, sems = refs[16:]
    token_ref[...] = tail_ref[:8, :]
    rstd, tail = rstd_ref[:, 0:1], tail_ref[:, 0:1]
    copies = []
    for q in range(4):
        dc = q % 2
        for dy in range(4):
            if q < 2:
                acc = lax.dot_general(
                    pair_ref[...], near[dc][dy][...], (((1,), (1,)), ((), ())), preferred_element_type=F32
                )
            else:
                acc = None
                for dx in range(4):
                    term = lax.dot_general(
                        pair_ref[:, aligned((where[0] + dx) % 4)],
                        far[dc][dx][dy * 256 : (dy + 1) * 256, :],
                        (((1,), (1,)), ((), ())),
                        preferred_element_type=F32,
                    )
                    acc = term if acc is None else acc + term
            cols = aligned(block_of(where, dy, q // 2, dc))
            out_ref[:, cols] = (
                acc * gain_ref[:, cols] * rstd - tok_ref[:, cols].astype(F32) * tail
            ).astype(BF16)
            copies.append(pltpu.make_async_copy(out_ref.at[:, cols], out_hbm.at[:, cols], sems.at[q * 4 + dy]))
            copies[-1].start()
    for copy in copies:
        copy.wait()


def backward(where, near, far, pair, tokens, rstd, tail, gain, ties=()):
    out = jax.ShapeDtypeStruct((512, 4096), BF16)
    return call(
        backward_kernel,
        "backward",
        4,
        where,
        (*near, *far, pair, tokens, rstd, tail, gain),
        [pltpu.HBM(out.shape, out.dtype), jax.ShapeDtypeStruct((8, 128), F32)],
        ties,
        [out],
        sems=(16,),
        out_hbm=True,
    )


def total(parts):
    acc = parts[0].astype(F32)
    for part in parts[1:]:
        acc = acc + part.astype(F32)
    return acc.astype(BF16)


def near_sum_kernel(where, *refs):
    for dx in range(4):
        rows = aligned((where[0] + dx) % 4)
        refs[5 + dx][...] = total([ref[rows, :] for ref in refs[:3]])
    refs[9][...] = refs[3][:128]
    refs[10][...] = refs[4][128:]


def far_sum_kernel(where, *refs):
    for dy in range(4):
        refs[4 + dy][...] = total([ref[dy] for ref in refs[:4]])


def sum_part(where, kernel, name, parts, ties=()):
    return call(kernel, name, 0, where, parts, [jax.ShapeDtypeStruct((256, 256), BF16)] * 4, ties)


def pair_sum_kernel(where, one_ref, other_ref, out_ref):
    out_ref[...] = total([one_ref[...], other_ref[...]])


def pair_sum(where, one, other, ties):
    outs = [jax.ShapeDtypeStruct(one.shape, BF16)]
    return call(pair_sum_kernel, "pair_sum", 0, where, (one, other), outs, ties)[0]


def last_kernel(where, *refs):
    for dx in range(4):
        got = refs[dx][...].astype(F32) * (1.0 / math.sqrt(131072))
        refs[4][:, aligned((where[0] + dx) % 4)] = got.T


def on_device(tokens, norm_gain, weight_values, weight_scales, grad_projected):
    replica, shard = lax.axis_index("replica"), lax.axis_index("shard")
    x, y, zh, core = replica // 4, shard // 4, shard // 2 % 2, shard % 2
    where = jnp.stack([x, y, zh, core]).astype(jnp.int32)
    gain = norm_gain[None, :]
    widened = jnp.repeat(weight_scales, 128, axis=1)
    own = (weight_values.astype(F32) * widened[:, None, :]).astype(BF16).reshape(256, 1024)

    rope = rope_tables(512, HD)
    with jax.named_scope("w_mirror"):
        quarter = to_mirror(lax.dynamic_slice(own, (0, x * 256), (256, 256)))
    held = [pltpu.with_memory_space_constraint(a, pltpu.HBM) for a in (tokens, grad_projected, gain, rope)]
    *normed, rstd, pair, pair_t, far_got = prologue(where, *held)
    with jax.named_scope("g_core_far"):
        far_got = to_core(far_got)
    near_got = other_near(where, pair_t, normed[1], (quarter,))
    *far_parts, sent = far_grad(where, pair_t, normed[2], far_got, own, (near_got,))
    with jax.named_scope("g_core_near"):
        near_got = to_core(near_got)
    with jax.named_scope("g_far_x"):
        far_parts = [far_parts[0]] + [to_x(far_parts[dx], dx) for dx in (1, 2, 3)]
    with jax.named_scope("w_near_y"):
        below, above = to_y(sent, 1), to_y(sent, -1)
    up, down, quarter = near_grad_first(where, pair_t, normed[0], near_got, quarter, (below, above))
    with jax.named_scope("g_near_y2"):
        up, down = to_y(up, 1), to_y(down, -1)
    with jax.named_scope("w_far_y"):
        quarters = [quarter] + [to_y(quarter, -dy) for dy in (1, 2, 3)]
    upper, lower, middle = near_grad_rest(
        where, pair_t, normed[0], near_got, up, down, (*far_parts[1:], *quarters)
    )
    with jax.named_scope("g_near_y"):
        near_parts = [middle, to_y(upper, 1), to_y(lower, -1)]
    pack = join(where, "join_far", quarters, (middle,))
    with jax.named_scope("w_far_x"):
        far = [pack] + [to_x(pack, -dx) for dx in (1, 2, 3)]
    outs = [jax.ShapeDtypeStruct((256, 256), BF16)] * 4 + [jax.ShapeDtypeStruct((128, 1024), BF16)] * 2
    args = (*near_parts, below, above)
    *near_cut, below_cut, above_cut = call(near_sum_kernel, "near_sum", 0, where, args, outs, (pack,))
    with jax.named_scope("w_near_y2"):
        across = (to_y(below_cut, 1), to_y(above_cut, -1))
    near = [own, above, join(where, "join_near", across, (near_cut[0],)), below]
    with jax.named_scope("w_near_core"):
        near = near + [to_core(a) for a in near]
    raw = forward_near(where, near, normed, (middle, pack))
    far_cut = sum_part(where, far_sum_kernel, "far_sum", far_parts, (near_cut[0], far[1], far[3]))
    with jax.named_scope("g_near_x"):
        near_cut = [near_cut[0]] + [to_x(near_cut[dx], dx) for dx in (1, 2, 3)]

    with jax.named_scope("w_far_core"):
        far = far + [to_core(a) for a in far]
    projected, tail = forward_far(where, far, normed, raw, pair, rstd, rope)
    grad_tokens, token = backward(where, near, far, pair, tokens, rstd, tail, gain)

    with jax.named_scope("g_far_y"):
        far_sum = total([far_cut[0]] + [to_y(far_cut[dy], dy) for dy in (1, 2, 3)])
    with jax.named_scope("g_mirror"):
        mine = total(near_cut + [to_mirror(far_sum)])
    with jax.named_scope("g_zlo1"):
        mine = total([mine, to_zlo(mine, 1)])
    with jax.named_scope("g_zlo3"):
        mine = pair_sum(where, mine, to_zlo(mine, 3), (tail,))
    with jax.named_scope("g_last_x"):
        quarters = [mine] + [to_x(mine, -dx) for dx in (1, 2, 3)]
    grad = call(last_kernel, "last", 0, where, quarters, [jax.ShapeDtypeStruct((256, 1024), F32)], (token,))[0]
    grad_weight = grad.reshape(2, 128, 1024)
    return (projected, grad_tokens, grad_weight)


def solution(mesh):
    return jax.shard_map(
        on_device,
        mesh=mesh,
        in_specs=(
            P(AXES, None),
            P(),
            P("shard", None, None),
            P("shard", None),
            P(AXES, None),
        ),
        out_specs=(
            P(AXES, None),
            P(AXES, None),
            P("shard", None, None),
        ),
        check_vma=False,
    )
```

```python
import math

import jax
import jax.numpy as jnp
import numpy as np
from jax import lax
from jax.experimental import pallas as pl
from jax.experimental.pallas import tpu as pltpu
from jax.sharding import PartitionSpec as P

HD = 128
AXES = ("replica", "shard")
F32 = jnp.float32
BF16 = jnp.bfloat16
NX, NY, NZL = 4, 4, 4


def place(device):
    replica, shard = divmod(device, 16)
    return replica // 4, shard // 4, (shard // 2 % 2) * 4 + replica % 4, shard % 2


def device_at(x, y, z, core):
    return ((x % 4) * 4 + z % 4) * 16 + (y % 4) * 4 + (z // 4) * 2 + core


def send(array, move):
    pairs = [(d, device_at(*move(*place(d)))) for d in range(256)]
    return lax.ppermute(array, AXES, pairs)


def to_x(array, step):
    return send(array, lambda x, y, z, c: (x + step, y, z, c))


def to_y(array, step):
    return send(array, lambda x, y, z, c: (x, y + step, z, c))


def to_core(array):
    return send(array, lambda x, y, z, c: (x, y, z, 1 - c))


def to_mirror(array):
    return send(array, lambda x, y, z, c: (x, y, 7 - z, c))


def to_zlo(array, flip):
    return send(array, lambda x, y, z, c: (x, y, (z // 4) * 4 + (z % 4 ^ flip), c))


def rope_tables(rows_here, head_size):
    half_size = head_size // 2
    position = np.arange(rows_here, dtype=np.float32)
    inverse = np.exp(-np.arange(half_size, dtype=np.float32) * np.float32(2.0 * math.log(500000.0) / head_size))
    angles = position[:, None] * inverse[None, :]
    cosine, sine = np.cos(angles), np.sin(angles)
    return jnp.asarray(np.concatenate([cosine, cosine, -sine, sine], axis=1), F32)


def block_of(where, dy, dzh, dc):
    y, zh, c = where[1], where[2], where[3]
    return ((y + dy) % 4) * 4 + (zh ^ dzh) * 2 + (c ^ dc)


def aligned(start):
    return pl.ds(pl.multiple_of(start * 256, 256), 256)


ROWS = 128


def prologue_kernel(where, tok_hbm, gproj_hbm, gain_hbm, rope_hbm, *refs):
    normed_refs, (rstd_ref, pair_ref, pair_t_ref, far_ref) = refs[:4], refs[4:8]
    tok_ref, gproj_ref, gain_ref, rope_ref, sems = refs[8:]
    small = [
        pltpu.make_async_copy(gain_hbm, gain_ref, sems.at[512 // ROWS, 0]),
        pltpu.make_async_copy(rope_hbm, rope_ref, sems.at[512 // ROWS, 1]),
    ]
    copies = []
    for i in range(512 // ROWS):
        rows = slice(i * ROWS, (i + 1) * ROWS)
        copies.append(pltpu.make_async_copy(tok_hbm.at[rows], tok_ref.at[rows], sems.at[i, 0]))
        copies.append(pltpu.make_async_copy(gproj_hbm.at[rows], gproj_ref.at[rows], sems.at[i, 1]))
    for copy in (*copies[:2], *small, *copies[2:]):
        copy.start()
    for copy in small:
        copy.wait()
    for i in range(512 // ROWS):
        rows = slice(i * ROWS, (i + 1) * ROWS)
        copies[2 * i].wait()
        copies[2 * i + 1].wait()
        total = jnp.zeros((ROWS, 128), F32)
        for b in range(32):
            part = tok_ref[rows, b * 128 : (b + 1) * 128].astype(F32)
            total = total + part * part
        rstd = lax.rsqrt(jnp.sum(total, axis=1, keepdims=True) * (1.0 / 4096) + 1e-05)
        rstd_ref[rows, :] = jnp.broadcast_to(rstd, (ROWS, 128))
        for q in range(4):
            for dy in range(4):
                cols = aligned(block_of(where, dy, q // 2, q % 2))
                part = tok_ref[rows, cols].astype(F32)
                normed_refs[q][rows, dy * 256 : (dy + 1) * 256] = (part * rstd * gain_ref[:, cols]).astype(BF16)
        for h in range(8):
            cols = slice(h * 128, (h + 1) * 128)
            pair = gproj_ref[rows, cols]
            if h < 4:
                g = pair.astype(F32)
                pair = (g * rope_ref[rows, :128] - pltpu.roll(g, 64, 1) * rope_ref[rows, 128:]).astype(BF16)
            pair_ref[rows, cols] = pair
            pair_t_ref[cols, rows] = pair.T
    other_grad_kernel(False, where, pair_t_ref, normed_refs[3], far_ref)


def prologue(where, tokens, gproj, gain, rope):
    outs = [jax.ShapeDtypeStruct((512, 1024), BF16)] * 4 + [
        jax.ShapeDtypeStruct((512, 128), F32),
        jax.ShapeDtypeStruct((512, 1024), BF16),
        jax.ShapeDtypeStruct((1024, 512), BF16),
        jax.ShapeDtypeStruct((4, 4, 256, 256), BF16),
    ]
    given = (tokens, gproj, gain, rope)
    scratch = [jax.ShapeDtypeStruct(a.shape, a.dtype) for a in given]
    return call(prologue_kernel, "prologue", 0, where, (), outs, (), scratch, given, (512 // ROWS + 1, 2))


def cost(products, mib):
    flops = products * 2 * 512 * 1024 * 1024
    return pl.CostEstimate(flops=flops, bytes_accessed=(mib << 20) if flops else 1024, transcendentals=0)


def call(kernel, name, products, where, args, outs, ties=(), scratch=(), hbm=(), sems=None, out_hbm=False):
    many, kept = len(args) + len(hbm), len(args) + len(hbm) + len(ties)
    size = sum(a.size * a.dtype.itemsize for a in scratch)

    def body(where, *refs):
        kernel(where, *refs[:many], *refs[kept:])

    return pl.pallas_call(
        body,
        in_specs=[pl.BlockSpec(memory_space=pltpu.SMEM)]
        + [pl.BlockSpec(memory_space=pltpu.VMEM)] * len(args)
        + [pl.BlockSpec(memory_space=pltpu.HBM)] * len(hbm)
        + [pl.BlockSpec(memory_space=pl.ANY)] * len(ties),
        out_specs=[
            pl.BlockSpec(memory_space=pltpu.HBM if out_hbm and i == 0 else pltpu.VMEM) for i in range(len(outs))
        ],
        out_shape=outs,
        scratch_shapes=[pltpu.VMEM(a.shape, a.dtype) for a in scratch]
        + ([] if sems is None else [pltpu.SemaphoreType.DMA(sems)]),
        compiler_params=pltpu.CompilerParams(vmem_limit_bytes=size + (8 << 20)),
        cost_estimate=cost(products, size >> 20),
        name=name,
    )(where, *args, *hbm, *ties)


def grad_block(where, pair_t_ref, n_ref, near, d):
    if near:
        return jnp.dot(pair_t_ref[...], n_ref[:, d * 256 : (d + 1) * 256], preferred_element_type=F32)
    return jnp.dot(pair_t_ref[aligned((where[0] + d) % 4), :], n_ref[...], preferred_element_type=F32)


def other_grad_kernel(near, where, pair_t_ref, n_ref, out_ref):
    for d in range(4):
        got = grad_block(where, pair_t_ref, n_ref, near, d)
        if near:
            out_ref[d] = got.astype(BF16)
        else:
            for dy in range(4):
                out_ref[d, dy] = got[:, dy * 256 : (dy + 1) * 256].astype(BF16)


def other_near(where, pair_t, normed, ties):
    outs = [jax.ShapeDtypeStruct((4, 1024, 256), BF16)]
    kernel = lambda *refs: other_grad_kernel(True, *refs)
    return call(kernel, "other_near", 40, where, (pair_t, normed), outs, ties)[0]


def far_grad_kernel(where, pair_t_ref, n_ref, got_ref, *refs):
    for dx in range(4):
        got = grad_block(where, pair_t_ref, n_ref, False, dx)
        for dy in range(4):
            part = got[:, dy * 256 : (dy + 1) * 256] + got_ref[dx, dy].astype(F32)
            refs[dx][dy] = part.astype(BF16)


def far_grad(where, pair_t, normed, got, ties):
    outs = [jax.ShapeDtypeStruct((4, 256, 256), BF16)] * 4
    return call(far_grad_kernel, "far_grad", 1, where, (pair_t, normed, got), outs, ties)


def near_grad_first_kernel(where, pair_t_ref, n_ref, got_ref, up_ref, down_ref):
    got = (grad_block(where, pair_t_ref, n_ref, True, 2) + got_ref[2].astype(F32)).astype(BF16)
    up_ref[...] = got[:512]
    down_ref[...] = got[512:]


def near_grad_first(where, pair_t, normed, got, ties):
    outs = [jax.ShapeDtypeStruct((512, 256), BF16)] * 2
    return call(near_grad_first_kernel, "near_grad_first", 0, where, (pair_t, normed, got), outs, ties)


def near_grad_rest_kernel(where, pair_t_ref, n_ref, got_ref, up_ref, down_ref, *refs):
    for slot, d in enumerate((1, 3, 0)):
        got = grad_block(where, pair_t_ref, n_ref, True, d) + got_ref[d].astype(F32)
        if d == 1:
            refs[slot][:512] = (got[:512] + up_ref[...].astype(F32)).astype(BF16)
            refs[slot][512:] = got[512:].astype(BF16)
        elif d == 3:
            refs[slot][:512] = got[:512].astype(BF16)
            refs[slot][512:] = (got[512:] + down_ref[...].astype(F32)).astype(BF16)
        else:
            refs[slot][...] = got.astype(BF16)


def near_grad_rest(where, pair_t, normed, got, up, down, ties):
    outs = [jax.ShapeDtypeStruct((1024, 256), BF16)] * 3
    return call(near_grad_rest_kernel, "near_grad_rest", 1, where, (pair_t, normed, got, up, down), outs, ties)


def join_kernel(where, *refs):
    start = 0
    for ref in refs[:-1]:
        refs[-1][start : start + ref.shape[0]] = ref[...]
        start += ref.shape[0]


def join(where, name, parts, ties=()):
    outs = [jax.ShapeDtypeStruct((sum(a.shape[0] for a in parts), parts[0].shape[1]), BF16)]
    return call(join_kernel, name, 0, where, parts, outs, ties)[0]


def forward_near_kernel(where, *refs):
    near, normed_refs, raw_ref = [refs[0:4], refs[4:8]], refs[8:10], refs[10]
    for n in range(4):
        cols = slice(n * 256, (n + 1) * 256)
        acc = None
        for dc in range(2):
            for dy in range(4):
                term = jnp.dot(
                    normed_refs[dc][:, dy * 256 : (dy + 1) * 256],
                    near[dc][dy][:, cols],
                    preferred_element_type=F32,
                )
                acc = term if acc is None else acc + term
        raw_ref[:, cols] = acc


def forward_near(where, near, normed, ties=()):
    outs = [jax.ShapeDtypeStruct((512, 1024), F32)]
    return call(forward_near_kernel, "forward_near", 2, where, (*near, *normed[:2]), outs, ties)[0]


def forward_far_kernel(where, *refs):
    far = [refs[0:4], refs[4:8]]
    normed_refs = refs[8:10]
    part_ref, pair_ref, rstd_ref, rope_ref, proj_ref, tail_ref, raw_ref = refs[10:]
    for dx in range(4):
        cols = aligned((where[0] + dx) % 4)
        acc = part_ref[:, cols]
        for dc in range(2):
            acc = acc + jnp.dot(normed_refs[dc][...], far[dc][dx][...], preferred_element_type=F32)
        raw_ref[:, cols] = acc
    dots = jnp.zeros((512, 128), F32)
    for n in range(8):
        cols = slice(n * 128, (n + 1) * 128)
        raw = raw_ref[:, cols]
        dots = dots + raw * pair_ref[:, cols].astype(F32)
        if n < 4:
            raw = raw * rope_ref[:, :128] + pltpu.roll(raw, 64, 1) * rope_ref[:, 128:]
        proj_ref[:, cols] = raw.astype(BF16)
    mean = jnp.sum(dots, axis=1, keepdims=True) * (1.0 / 4096)
    tail_ref[...] = mean * rstd_ref[...] * rstd_ref[...]


def forward_far(where, far, normed, part, pair, rstd, rope, ties=()):
    raw = jax.ShapeDtypeStruct((512, 1024), F32)
    return call(
        forward_far_kernel,
        "forward_far",
        2,
        where,
        (*far, *normed[2:], part, pair, rstd, rope),
        [jax.ShapeDtypeStruct((512, 1024), BF16), jax.ShapeDtypeStruct((512, 128), F32)],
        ties,
        [raw],
    )


def backward_kernel(where, *refs):
    near, far = [refs[0:4], refs[4:8]], [refs[8:12], refs[12:16]]
    pair_ref, tok_ref, rstd_ref, tail_ref, gain_ref, out_hbm, token_ref, out_ref, sems = refs[16:]
    token_ref[...] = tail_ref[:8, :]
    rstd, tail = rstd_ref[:, 0:1], tail_ref[:, 0:1]
    copies = []
    for q in range(4):
        dc = q % 2
        for dy in range(4):
            if q < 2:
                acc = lax.dot_general(
                    pair_ref[...], near[dc][dy][...], (((1,), (1,)), ((), ())), preferred_element_type=F32
                )
            else:
                acc = None
                for dx in range(4):
                    term = lax.dot_general(
                        pair_ref[:, aligned((where[0] + dx) % 4)],
                        far[dc][dx][dy * 256 : (dy + 1) * 256, :],
                        (((1,), (1,)), ((), ())),
                        preferred_element_type=F32,
                    )
                    acc = term if acc is None else acc + term
            cols = aligned(block_of(where, dy, q // 2, dc))
            out_ref[:, cols] = (
                acc * gain_ref[:, cols] * rstd - tok_ref[:, cols].astype(F32) * tail
            ).astype(BF16)
            copies.append(pltpu.make_async_copy(out_ref.at[:, cols], out_hbm.at[:, cols], sems.at[q * 4 + dy]))
            copies[-1].start()
    for copy in copies:
        copy.wait()


def backward(where, near, far, pair, tokens, rstd, tail, gain, ties=()):
    out = jax.ShapeDtypeStruct((512, 4096), BF16)
    return call(
        backward_kernel,
        "backward",
        4,
        where,
        (*near, *far, pair, tokens, rstd, tail, gain),
        [pltpu.HBM(out.shape, out.dtype), jax.ShapeDtypeStruct((8, 128), F32)],
        ties,
        [out],
        sems=(16,),
        out_hbm=True,
    )


def total(parts):
    acc = parts[0].astype(F32)
    for part in parts[1:]:
        acc = acc + part.astype(F32)
    return acc.astype(BF16)


def near_sum_kernel(where, *refs):
    for dx in range(4):
        rows = aligned((where[0] + dx) % 4)
        refs[5 + dx][...] = total([ref[rows, :] for ref in refs[:3]])
    refs[9][...] = refs[3][:128]
    refs[10][...] = refs[4][128:]


def far_sum_kernel(where, *refs):
    for dy in range(4):
        refs[4 + dy][...] = total([ref[dy] for ref in refs[:4]])


def sum_part(where, kernel, name, parts, ties=()):
    return call(kernel, name, 0, where, parts, [jax.ShapeDtypeStruct((256, 256), BF16)] * 4, ties)


def pair_sum_kernel(where, one_ref, other_ref, out_ref):
    out_ref[...] = total([one_ref[...], other_ref[...]])


def pair_sum(where, one, other, ties):
    outs = [jax.ShapeDtypeStruct(one.shape, BF16)]
    return call(pair_sum_kernel, "pair_sum", 0, where, (one, other), outs, ties)[0]


def last_kernel(where, *refs):
    for dx in range(4):
        got = refs[dx][...].astype(F32) * (1.0 / math.sqrt(131072))
        refs[4][:, aligned((where[0] + dx) % 4)] = got.T


def on_device(tokens, norm_gain, weight_values, weight_scales, grad_projected):
    replica, shard = lax.axis_index("replica"), lax.axis_index("shard")
    x, y, zh, core = replica // 4, shard // 4, shard // 2 % 2, shard % 2
    where = jnp.stack([x, y, zh, core]).astype(jnp.int32)
    gain = norm_gain[None, :]
    widened = jnp.repeat(weight_scales, 128, axis=1)
    own = (weight_values.astype(F32) * widened[:, None, :]).astype(BF16).reshape(256, 1024)

    rope = rope_tables(512, HD)
    with jax.named_scope("w_mirror"):
        quarter = to_mirror(lax.dynamic_slice(own, (0, x * 256), (256, 256)))
    held = [pltpu.with_memory_space_constraint(a, pltpu.HBM) for a in (tokens, grad_projected, gain, rope)]
    *normed, rstd, pair, pair_t, far_got = prologue(where, *held)
    with jax.named_scope("g_core_far"):
        far_got = to_core(far_got)
    with jax.named_scope("w_near_y"):
        below, above = to_y(own, 1), to_y(own, -1)
    near_got = other_near(where, pair_t, normed[1], (quarter, below, above))
    far_parts = far_grad(where, pair_t, normed[2], far_got, (near_got,))
    with jax.named_scope("g_core_near"):
        near_got = to_core(near_got)
    with jax.named_scope("g_far_x"):
        far_parts = [far_parts[0]] + [to_x(far_parts[dx], dx) for dx in (1, 2, 3)]
    up, down = near_grad_first(where, pair_t, normed[0], near_got, (far_parts[0],))
    with jax.named_scope("g_near_y2"):
        up, down = to_y(up, 1), to_y(down, -1)
    quarter = join(where, "pass_quarter", [quarter], (up, down))
    with jax.named_scope("w_far_y"):
        quarters = [quarter] + [to_y(quarter, -dy) for dy in (1, 2, 3)]
    upper, lower, middle = near_grad_rest(
        where, pair_t, normed[0], near_got, up, down, (*far_parts[1:], *quarters)
    )
    with jax.named_scope("g_near_y"):
        near_parts = [middle, to_y(upper, 1), to_y(lower, -1)]
    pack = join(where, "join_far", quarters, (middle,))
    with jax.named_scope("w_far_x"):
        far = [pack] + [to_x(pack, -dx) for dx in (1, 2, 3)]
    outs = [jax.ShapeDtypeStruct((256, 256), BF16)] * 4 + [jax.ShapeDtypeStruct((128, 1024), BF16)] * 2
    args = (*near_parts, below, above)
    *near_cut, below_cut, above_cut = call(near_sum_kernel, "near_sum", 0, where, args, outs, (pack,))
    with jax.named_scope("w_near_y2"):
        across = (to_y(below_cut, 1), to_y(above_cut, -1))
    near = [own, above, join(where, "join_near", across, (near_cut[0],)), below]
    with jax.named_scope("w_near_core"):
        near = near + [to_core(a) for a in near]
    raw = forward_near(where, near, normed, (middle, pack))
    far_cut = sum_part(where, far_sum_kernel, "far_sum", far_parts, (near_cut[0], far[1], far[3]))
    with jax.named_scope("g_near_x"):
        near_cut = [near_cut[0]] + [to_x(near_cut[dx], dx) for dx in (1, 2, 3)]

    with jax.named_scope("w_far_core"):
        far = far + [to_core(a) for a in far]
    projected, tail = forward_far(where, far, normed, raw, pair, rstd, rope)
    grad_tokens, token = backward(where, near, far, pair, tokens, rstd, tail, gain)

    with jax.named_scope("g_far_y"):
        far_sum = total([far_cut[0]] + [to_y(far_cut[dy], dy) for dy in (1, 2, 3)])
    with jax.named_scope("g_mirror"):
        mine = total(near_cut + [to_mirror(far_sum)])
    with jax.named_scope("g_zlo1"):
        mine = total([mine, to_zlo(mine, 1)])
    with jax.named_scope("g_zlo3"):
        mine = pair_sum(where, mine, to_zlo(mine, 3), (tail,))
    with jax.named_scope("g_last_x"):
        quarters = [mine] + [to_x(mine, -dx) for dx in (1, 2, 3)]
    grad = call(last_kernel, "last", 0, where, quarters, [jax.ShapeDtypeStruct((256, 1024), F32)], (token,))[0]
    grad_weight = grad.reshape(2, 128, 1024)
    return (projected, grad_tokens, grad_weight)


def solution(mesh):
    return jax.shard_map(
        on_device,
        mesh=mesh,
        in_specs=(
            P(AXES, None),
            P(),
            P("shard", None, None),
            P("shard", None),
            P(AXES, None),
        ),
        out_specs=(
            P(AXES, None),
            P(AXES, None),
            P("shard", None, None),
        ),
        check_vma=False,
    )
```

```python
import math

import jax
import jax.numpy as jnp
import numpy as np
from jax import lax
from jax.experimental import pallas as pl
from jax.experimental.pallas import tpu as pltpu
from jax.sharding import PartitionSpec as P

HD = 128
AXES = ("replica", "shard")
F32 = jnp.float32
BF16 = jnp.bfloat16
NX, NY, NZL = 4, 4, 4


def place(device):
    replica, shard = divmod(device, 16)
    return replica // 4, shard // 4, (shard // 2 % 2) * 4 + replica % 4, shard % 2


def device_at(x, y, z, core):
    return ((x % 4) * 4 + z % 4) * 16 + (y % 4) * 4 + (z // 4) * 2 + core


def send(array, move):
    pairs = [(d, device_at(*move(*place(d)))) for d in range(256)]
    return lax.ppermute(array, AXES, pairs)


def to_x(array, step):
    return send(array, lambda x, y, z, c: (x + step, y, z, c))


def to_y(array, step):
    return send(array, lambda x, y, z, c: (x, y + step, z, c))


def to_core(array):
    return send(array, lambda x, y, z, c: (x, y, z, 1 - c))


def to_mirror(array):
    return send(array, lambda x, y, z, c: (x, y, 7 - z, c))


def to_zlo(array, flip):
    return send(array, lambda x, y, z, c: (x, y, (z // 4) * 4 + (z % 4 ^ flip), c))


def rope_tables(rows_here, head_size):
    half_size = head_size // 2
    position = np.arange(rows_here, dtype=np.float32)
    inverse = np.exp(-np.arange(half_size, dtype=np.float32) * np.float32(2.0 * math.log(500000.0) / head_size))
    angles = position[:, None] * inverse[None, :]
    cosine, sine = np.cos(angles), np.sin(angles)
    return jnp.asarray(np.concatenate([cosine, cosine, -sine, sine], axis=1), F32)


def block_of(where, dy, dzh, dc):
    y, zh, c = where[1], where[2], where[3]
    return ((y + dy) % 4) * 4 + (zh ^ dzh) * 2 + (c ^ dc)


def aligned(start):
    return pl.ds(pl.multiple_of(start * 256, 256), 256)


ROWS = 128


def prologue_kernel(where, tok_hbm, gproj_hbm, gain_hbm, rope_hbm, *refs):
    normed_refs, (rstd_ref, pair_ref, pair_t_ref, far_ref) = refs[:4], refs[4:8]
    tok_ref, gproj_ref, gain_ref, rope_ref, sems = refs[8:]
    small = [
        pltpu.make_async_copy(gain_hbm, gain_ref, sems.at[512 // ROWS, 0]),
        pltpu.make_async_copy(rope_hbm, rope_ref, sems.at[512 // ROWS, 1]),
    ]
    copies = []
    for i in range(512 // ROWS):
        rows = slice(i * ROWS, (i + 1) * ROWS)
        copies.append(pltpu.make_async_copy(tok_hbm.at[rows], tok_ref.at[rows], sems.at[i, 0]))
        copies.append(pltpu.make_async_copy(gproj_hbm.at[rows], gproj_ref.at[rows], sems.at[i, 1]))
    for copy in (*copies[:2], *small, *copies[2:]):
        copy.start()
    for copy in small:
        copy.wait()
    for i in range(512 // ROWS):
        rows = slice(i * ROWS, (i + 1) * ROWS)
        copies[2 * i].wait()
        copies[2 * i + 1].wait()
        total = jnp.zeros((ROWS, 128), F32)
        for b in range(32):
            part = tok_ref[rows, b * 128 : (b + 1) * 128].astype(F32)
            total = total + part * part
        rstd = lax.rsqrt(jnp.sum(total, axis=1, keepdims=True) * (1.0 / 4096) + 1e-05)
        rstd_ref[rows, :] = jnp.broadcast_to(rstd, (ROWS, 128))
        for q in range(4):
            for dy in range(4):
                cols = aligned(block_of(where, dy, q // 2, q % 2))
                part = tok_ref[rows, cols].astype(F32)
                normed_refs[q][rows, dy * 256 : (dy + 1) * 256] = (part * rstd * gain_ref[:, cols]).astype(BF16)
        for h in range(8):
            cols = slice(h * 128, (h + 1) * 128)
            pair = gproj_ref[rows, cols]
            if h < 4:
                g = pair.astype(F32)
                pair = (g * rope_ref[rows, :128] - pltpu.roll(g, 64, 1) * rope_ref[rows, 128:]).astype(BF16)
            pair_ref[rows, cols] = pair
            pair_t_ref[cols, rows] = pair.T
    other_grad_kernel(False, where, pair_t_ref, normed_refs[3], far_ref)


def prologue(where, tokens, gproj, gain, rope):
    outs = [jax.ShapeDtypeStruct((512, 1024), BF16)] * 4 + [
        jax.ShapeDtypeStruct((512, 128), F32),
        jax.ShapeDtypeStruct((512, 1024), BF16),
        jax.ShapeDtypeStruct((1024, 512), BF16),
        jax.ShapeDtypeStruct((4, 4, 256, 256), BF16),
    ]
    given = (tokens, gproj, gain, rope)
    scratch = [jax.ShapeDtypeStruct(a.shape, a.dtype) for a in given]
    return call(prologue_kernel, "prologue", 0, where, (), outs, (), scratch, given, (512 // ROWS + 1, 2))


def cost(products, mib):
    flops = products * 2 * 512 * 1024 * 1024
    return pl.CostEstimate(flops=flops, bytes_accessed=(mib << 20) if flops else 1024, transcendentals=0)


def call(kernel, name, products, where, args, outs, ties=(), scratch=(), hbm=(), sems=None, out_hbm=False):
    many, kept = len(args) + len(hbm), len(args) + len(hbm) + len(ties)
    size = sum(a.size * a.dtype.itemsize for a in scratch)

    def body(where, *refs):
        kernel(where, *refs[:many], *refs[kept:])

    return pl.pallas_call(
        body,
        in_specs=[pl.BlockSpec(memory_space=pltpu.SMEM)]
        + [pl.BlockSpec(memory_space=pltpu.VMEM)] * len(args)
        + [pl.BlockSpec(memory_space=pltpu.HBM)] * len(hbm)
        + [pl.BlockSpec(memory_space=pl.ANY)] * len(ties),
        out_specs=[
            pl.BlockSpec(memory_space=pltpu.HBM if out_hbm and i == 0 else pltpu.VMEM) for i in range(len(outs))
        ],
        out_shape=outs,
        scratch_shapes=[pltpu.VMEM(a.shape, a.dtype) for a in scratch]
        + ([] if sems is None else [pltpu.SemaphoreType.DMA(sems)]),
        compiler_params=pltpu.CompilerParams(vmem_limit_bytes=size + (8 << 20)),
        cost_estimate=cost(products, size >> 20),
        name=name,
    )(where, *args, *hbm, *ties)


def grad_block(where, pair_t_ref, n_ref, near, d):
    if near:
        return jnp.dot(pair_t_ref[...], n_ref[:, d * 256 : (d + 1) * 256], preferred_element_type=F32)
    return jnp.dot(pair_t_ref[aligned((where[0] + d) % 4), :], n_ref[...], preferred_element_type=F32)


def other_grad_kernel(near, where, pair_t_ref, n_ref, out_ref):
    for d in range(4):
        got = grad_block(where, pair_t_ref, n_ref, near, d)
        if near:
            out_ref[d] = got.astype(BF16)
        else:
            for dy in range(4):
                out_ref[d, dy] = got[:, dy * 256 : (dy + 1) * 256].astype(BF16)


def other_near(where, pair_t, normed, ties):
    outs = [jax.ShapeDtypeStruct((4, 1024, 256), BF16)]
    kernel = lambda *refs: other_grad_kernel(True, *refs)
    return call(kernel, "other_near", 40, where, (pair_t, normed), outs, ties)[0]


def far_grad_kernel(where, pair_t_ref, n_ref, got_ref, *refs):
    for dx in range(4):
        got = grad_block(where, pair_t_ref, n_ref, False, dx)
        for dy in range(4):
            part = got[:, dy * 256 : (dy + 1) * 256] + got_ref[dx, dy].astype(F32)
            refs[dx][dy] = part.astype(BF16)


def far_grad(where, pair_t, normed, got, ties):
    outs = [jax.ShapeDtypeStruct((4, 256, 256), BF16)] * 4
    return call(far_grad_kernel, "far_grad", 1, where, (pair_t, normed, got), outs, ties)


def near_grad_first_kernel(where, pair_t_ref, n_ref, got_ref, up_ref, down_ref):
    got = (grad_block(where, pair_t_ref, n_ref, True, 2) + got_ref[2].astype(F32)).astype(BF16)
    up_ref[...] = got[:512]
    down_ref[...] = got[512:]


def near_grad_first(where, pair_t, normed, got, ties):
    outs = [jax.ShapeDtypeStruct((512, 256), BF16)] * 2
    return call(near_grad_first_kernel, "near_grad_first", 0, where, (pair_t, normed, got), outs, ties)


def near_grad_rest_kernel(where, pair_t_ref, n_ref, got_ref, up_ref, down_ref, *refs):
    for slot, d in enumerate((1, 3, 0)):
        got = grad_block(where, pair_t_ref, n_ref, True, d) + got_ref[d].astype(F32)
        if d == 1:
            refs[slot][:512] = (got[:512] + up_ref[...].astype(F32)).astype(BF16)
            refs[slot][512:] = got[512:].astype(BF16)
        elif d == 3:
            refs[slot][:512] = got[:512].astype(BF16)
            refs[slot][512:] = (got[512:] + down_ref[...].astype(F32)).astype(BF16)
        else:
            refs[slot][...] = got.astype(BF16)


def near_grad_rest(where, pair_t, normed, got, up, down, ties):
    outs = [jax.ShapeDtypeStruct((1024, 256), BF16)] * 3
    return call(near_grad_rest_kernel, "near_grad_rest", 1, where, (pair_t, normed, got, up, down), outs, ties)


def join_kernel(where, *refs):
    start = 0
    for ref in refs[:-1]:
        refs[-1][start : start + ref.shape[0]] = ref[...]
        start += ref.shape[0]


def join(where, name, parts, ties=()):
    outs = [jax.ShapeDtypeStruct((sum(a.shape[0] for a in parts), parts[0].shape[1]), BF16)]
    return call(join_kernel, name, 0, where, parts, outs, ties)[0]


def forward_near_kernel(where, *refs):
    near, normed_refs, raw_ref = [refs[0:4], refs[4:8]], refs[8:10], refs[10]
    for n in range(4):
        cols = slice(n * 256, (n + 1) * 256)
        acc = None
        for dc in range(2):
            for dy in range(4):
                term = jnp.dot(
                    normed_refs[dc][:, dy * 256 : (dy + 1) * 256],
                    near[dc][dy][:, cols],
                    preferred_element_type=F32,
                )
                acc = term if acc is None else acc + term
        raw_ref[:, cols] = acc


def forward_near(where, near, normed, ties=()):
    outs = [jax.ShapeDtypeStruct((512, 1024), F32)]
    return call(forward_near_kernel, "forward_near", 2, where, (*near, *normed[:2]), outs, ties)[0]


def forward_far_kernel(where, *refs):
    far = [refs[0:4], refs[4:8]]
    normed_refs = refs[8:10]
    part_ref, pair_ref, rstd_ref, rope_ref, proj_ref, tail_ref, raw_ref = refs[10:]
    for dx in range(4):
        cols = aligned((where[0] + dx) % 4)
        acc = part_ref[:, cols]
        for dc in range(2):
            acc = acc + jnp.dot(normed_refs[dc][...], far[dc][dx][...], preferred_element_type=F32)
        raw_ref[:, cols] = acc
    dots = jnp.zeros((512, 128), F32)
    for n in range(8):
        cols = slice(n * 128, (n + 1) * 128)
        raw = raw_ref[:, cols]
        dots = dots + raw * pair_ref[:, cols].astype(F32)
        if n < 4:
            raw = raw * rope_ref[:, :128] + pltpu.roll(raw, 64, 1) * rope_ref[:, 128:]
        proj_ref[:, cols] = raw.astype(BF16)
    mean = jnp.sum(dots, axis=1, keepdims=True) * (1.0 / 4096)
    tail_ref[...] = mean * rstd_ref[...] * rstd_ref[...]


def forward_far(where, far, normed, part, pair, rstd, rope, ties=()):
    raw = jax.ShapeDtypeStruct((512, 1024), F32)
    return call(
        forward_far_kernel,
        "forward_far",
        2,
        where,
        (*far, *normed[2:], part, pair, rstd, rope),
        [jax.ShapeDtypeStruct((512, 1024), BF16), jax.ShapeDtypeStruct((512, 128), F32)],
        ties,
        [raw],
    )


def backward_kernel(where, *refs):
    near, far = [refs[0:4], refs[4:8]], [refs[8:12], refs[12:16]]
    pair_ref, tok_ref, rstd_ref, tail_ref, gain_ref, out_hbm, token_ref, out_ref, sems = refs[16:]
    token_ref[...] = tail_ref[:8, :]
    rstd, tail = rstd_ref[:, 0:1], tail_ref[:, 0:1]
    copies = []
    for q in range(4):
        dc = q % 2
        for dy in range(4):
            if q < 2:
                acc = lax.dot_general(
                    pair_ref[...], near[dc][dy][...], (((1,), (1,)), ((), ())), preferred_element_type=F32
                )
            else:
                acc = None
                for dx in range(4):
                    term = lax.dot_general(
                        pair_ref[:, aligned((where[0] + dx) % 4)],
                        far[dc][dx][dy * 256 : (dy + 1) * 256, :],
                        (((1,), (1,)), ((), ())),
                        preferred_element_type=F32,
                    )
                    acc = term if acc is None else acc + term
            cols = aligned(block_of(where, dy, q // 2, dc))
            out_ref[:, cols] = (
                acc * gain_ref[:, cols] * rstd - tok_ref[:, cols].astype(F32) * tail
            ).astype(BF16)
            copies.append(pltpu.make_async_copy(out_ref.at[:, cols], out_hbm.at[:, cols], sems.at[q * 4 + dy]))
            copies[-1].start()
    for copy in copies:
        copy.wait()


def backward(where, near, far, pair, tokens, rstd, tail, gain, ties=()):
    out = jax.ShapeDtypeStruct((512, 4096), BF16)
    return call(
        backward_kernel,
        "backward",
        4,
        where,
        (*near, *far, pair, tokens, rstd, tail, gain),
        [pltpu.HBM(out.shape, out.dtype), jax.ShapeDtypeStruct((8, 128), F32)],
        ties,
        [out],
        sems=(16,),
        out_hbm=True,
    )


def total(parts):
    acc = parts[0].astype(F32)
    for part in parts[1:]:
        acc = acc + part.astype(F32)
    return acc.astype(BF16)


def near_sum_kernel(where, *refs):
    for dx in range(4):
        rows = aligned((where[0] + dx) % 4)
        refs[5 + dx][...] = total([ref[rows, :] for ref in refs[:3]])
    refs[9][...] = refs[3][:128]
    refs[10][...] = refs[4][128:]


def far_sum_kernel(where, *refs):
    for dy in range(4):
        refs[4 + dy][...] = total([ref[dy] for ref in refs[:4]])


def sum_part(where, kernel, name, parts, ties=()):
    return call(kernel, name, 0, where, parts, [jax.ShapeDtypeStruct((256, 256), BF16)] * 4, ties)


def pair_sum_kernel(where, one_ref, other_ref, out_ref):
    out_ref[...] = total([one_ref[...], other_ref[...]])


def pair_sum(where, one, other, ties):
    outs = [jax.ShapeDtypeStruct(one.shape, BF16)]
    return call(pair_sum_kernel, "pair_sum", 0, where, (one, other), outs, ties)[0]


def last_kernel(where, *refs):
    for dx in range(4):
        got = refs[dx][...].astype(F32) * (1.0 / math.sqrt(131072))
        refs[4][:, aligned((where[0] + dx) % 4)] = got.T


def on_device(tokens, norm_gain, weight_values, weight_scales, grad_projected):
    replica, shard = lax.axis_index("replica"), lax.axis_index("shard")
    x, y, zh, core = replica // 4, shard // 4, shard // 2 % 2, shard % 2
    where = jnp.stack([x, y, zh, core]).astype(jnp.int32)
    gain = norm_gain[None, :]
    widened = jnp.repeat(weight_scales, 128, axis=1)
    own = (weight_values.astype(F32) * widened[:, None, :]).astype(BF16).reshape(256, 1024)

    rope = rope_tables(512, HD)
    with jax.named_scope("w_mirror"):
        quarter = to_mirror(lax.dynamic_slice(own, (0, x * 256), (256, 256)))
    held = [pltpu.with_memory_space_constraint(a, pltpu.HBM) for a in (tokens, grad_projected, gain, rope)]
    *normed, rstd, pair, pair_t, far_got = prologue(where, *held)
    with jax.named_scope("g_core_far"):
        far_got = to_core(far_got)
    with jax.named_scope("w_near_y"):
        below, above = to_y(own, 1), to_y(own, -1)
    near_got = other_near(where, pair_t, normed[1], (quarter, below, above))
    far_parts = far_grad(where, pair_t, normed[2], far_got, (near_got,))
    with jax.named_scope("g_core_near"):
        near_got = to_core(near_got)
    with jax.named_scope("g_far_x"):
        far_parts = [far_parts[0]] + [to_x(far_parts[dx], dx) for dx in (1, 2, 3)]
    up, down = near_grad_first(where, pair_t, normed[0], near_got, (far_parts[0],))
    with jax.named_scope("g_near_y2"):
        up, down = to_y(up, 1), to_y(down, -1)
    quarter = join(where, "pass_quarter", [quarter], (up, down))
    with jax.named_scope("w_far_y"):
        quarters = [quarter] + [to_y(quarter, -dy) for dy in (1, 2, 3)]
    far_cut = sum_part(where, far_sum_kernel, "far_sum", far_parts, quarters[1:])
    with jax.named_scope("g_far_y"):
        far_cut = [far_cut[0]] + [to_y(far_cut[dy], dy) for dy in (1, 2, 3)]
        far_sum = total(far_cut)
    with jax.named_scope("g_mirror"):
        mirrored = to_mirror(far_sum)
    upper, lower, middle = near_grad_rest(where, pair_t, normed[0], near_got, up, down, far_cut[1:])
    with jax.named_scope("g_near_y"):
        near_parts = [middle, to_y(upper, 1), to_y(lower, -1)]
    pack = join(where, "join_far", quarters, (far_cut[0],))
    with jax.named_scope("w_far_x"):
        far = [pack, to_x(pack, -1), None, to_x(pack, -3)]
    outs = [jax.ShapeDtypeStruct((256, 256), BF16)] * 4 + [jax.ShapeDtypeStruct((128, 1024), BF16)] * 2
    args = (*near_parts, below, above)
    *near_cut, below_cut, above_cut = call(near_sum_kernel, "near_sum", 0, where, args, outs, (far[1], far[3], mirrored))
    with jax.named_scope("w_near_y2"):
        across = (to_y(below_cut, 1), to_y(above_cut, -1))
    near = [own, above, join(where, "join_near", across, (near_cut[0],)), below]
    with jax.named_scope("w_near_core"):
        near = near + [to_core(a) for a in near]
    raw = forward_near(where, near, normed, (middle, pack))
    with jax.named_scope("g_near_x"):
        near_cut = [near_cut[0]] + [to_x(near_cut[dx], dx) for dx in (1, 2, 3)]
    passed = join(where, "pass_pack", [pack], near_cut[1:])
    with jax.named_scope("w_far_x2"):
        far[2] = to_x(passed, -2)
    with jax.named_scope("w_far_core"):
        far = far + [to_core(a) for a in far]
    projected, tail = forward_far(where, far, normed, raw, pair, rstd, rope)
    grad_tokens, token = backward(where, near, far, pair, tokens, rstd, tail, gain)

    mine = total(near_cut + [mirrored])
    with jax.named_scope("g_zlo1"):
        mine = total([mine, to_zlo(mine, 1)])
    with jax.named_scope("g_zlo3"):
        mine = pair_sum(where, mine, to_zlo(mine, 3), (tail,))
    with jax.named_scope("g_last_x"):
        quarters = [mine] + [to_x(mine, -dx) for dx in (1, 2, 3)]
    grad = call(last_kernel, "last", 0, where, quarters, [jax.ShapeDtypeStruct((256, 1024), F32)], (token,))[0]
    grad_weight = grad.reshape(2, 128, 1024)
    return (projected, grad_tokens, grad_weight)


def solution(mesh):
    return jax.shard_map(
        on_device,
        mesh=mesh,
        in_specs=(
            P(AXES, None),
            P(),
            P("shard", None, None),
            P("shard", None),
            P(AXES, None),
        ),
        out_specs=(
            P(AXES, None),
            P(AXES, None),
            P("shard", None, None),
        ),
        check_vma=False,
    )
```
